32 devices in a mesh: ax: 16 (over z, y, x), rad: 2 (over core).
Axes of the slice: x: 2, y: 2, z: 4, core: 2. Of those that a mesh axis runs over, the one named last changes fastest.
Arguments:
- fields: float32 [128, 5, 8, 1024], P('ax', None, None, 'rad'), may hold values from -6 to 6
Outputs:
- axial_deriv: float32 [128, 5, 8, 1024], P('ax', None, None, 'rad')
- filtered: float32 [128, 5, 8, 1024], P('ax', None, None, 'rad')
- radial_deriv: float32 [128, 5, 8, 1024], P('ax', None, None, 'rad')
The draws below stay inside these ranges and needn't reach their ends.
All inputs are finite; a program needn't handle non-finite values.
Results may differ from the reference program's by a relative error of at most 0.0003.
Values sent between devices are 32-bit elements; how exact they have to be, the bound alone decides.
A program may use at most 128 MiB of HBM per device.

```python
import jax
import jax.numpy as jnp
from jax import lax

NR = 1024
PLANES = 8
FIELDS = 5
NA = 128


def block_scale(stream_key, shape, shards, low, largest):
    def one(axis_at, parts):
        heights = jax.random.uniform(jax.random.fold_in(jax.random.fold_in(stream_key, 6), axis_at), (parts,), jnp.float32, low / len(shards), largest / len(shards))
        return jnp.repeat(jnp.exp(heights), shape[axis_at] // parts).reshape((-1,) + (1,) * (len(shape) - axis_at - 1))

    level = one(*shards[0])
    for cut in shards[1:]:
        level = level * one(*cut)
    return level


def centred(rng, dims, width, limit, shards=(), held_as=jnp.bfloat16):
    result = jax.random.normal(rng, dims, jnp.float32) * width
    if len(shards) > 0:
        result = block_scale(rng, dims, shards, -0.22, 0.18) * result
    return jnp.clip(result, min=-limit, max=limit).astype(held_as)


def setup_inputs(seed: int = 0) -> dict:
    seeds = jax.random.split(jax.random.key(seed), 2)
    return {
        "fields": centred(seeds[0], (NA, FIELDS, PLANES, NR), 1.0, 6.0, ((0, 16), (3, 2)), jnp.float32),
    }


deriv_alpha = 1.0 / 3.0
filter_alpha = 0.4999

def filter_weights():
    af = filter_alpha
    return [(93.0 + 70.0 * af) / 128.0, (7.0 + 18.0 * af) / 16.0, (-7.0 + 14.0 * af) / 32.0, (1.0 - 2.0 * af) / 16.0, (-1.0 + 2.0 * af) / 128.0]

def line_solve(alpha, rhs):
    count = rhs.shape[0]
    flat = rhs.reshape(count, -1)
    lower = jnp.full((count,), alpha, rhs.dtype).at[0].set(0.0)
    upper = jnp.full((count,), alpha, rhs.dtype).at[count - 1].set(0.0)
    diag = jnp.ones((count,), rhs.dtype)
    return lax.linalg.tridiagonal_solve(lower, diag, upper, flat).reshape(rhs.shape)

def one_field(field):
    count = field.shape[0]
    radial = field.shape[2]
    padded = jnp.pad(field, ((4, 4), (0, 0), (0, 0)))

    def shifted(k):
        return padded[4 + k:4 + k + count]
    deriv_rhs = 7.0 / 9.0 * (shifted(1) - shifted(-1)) + 1.0 / 36.0 * (shifted(2) - shifted(-2))
    weights = filter_weights()
    filter_rhs = weights[0] * shifted(0)
    for n in range(1, 5):
        filter_rhs = filter_rhs + weights[n] / 2.0 * (shifted(n) + shifted(-n))
    axial_deriv = line_solve(deriv_alpha, deriv_rhs)
    filtered = line_solve(filter_alpha, filter_rhs)
    rpad = jnp.pad(field, ((0, 0), (0, 0), (3, 3)))

    def radial_cell(k):
        return rpad[:, :, 3 + k:3 + k + radial]
    radial_deriv = (45.0 * (radial_cell(1) - radial_cell(-1)) - 9.0 * (radial_cell(2) - radial_cell(-2)) + (radial_cell(3) - radial_cell(-3))) / 60.0
    return (axial_deriv, filtered, radial_deriv)

def reference(fields):
    moved = jnp.moveaxis(fields, 1, 0)
    axial_deriv, filtered, radial_deriv = lax.map(one_field, moved)
    return (jnp.moveaxis(axial_deriv, 0, 1), jnp.moveaxis(filtered, 0, 1), jnp.moveaxis(radial_deriv, 0, 1))
```

```python
import functools

import jax
import jax.numpy as jnp
import numpy as np
from jax import lax
from jax.experimental import pallas as pl
from jax.experimental.pallas import tpu as pltpu
from jax.sharding import PartitionSpec as P

MESH = pl.DeviceIdType.MESH
ALPHAS = (1.0 / 3.0, 0.4999)
HALO = 3
EDGE = 128


def stage_radices(n):
    radices, m = [], n
    for _ in range(2):
        if m % 2 == 0 and m > 2:
            radices.append(2)
            m //= 2
    while m > 8:
        radix = next(k for k in (4, 2, 3, 5, 7, m) if m % k == 0)
        radices.append(radix)
        m //= radix
    if m > 1:
        radices.append(m)
    return radices


def stencils():
    af = ALPHAS[1]
    a = [
        (93.0 + 70.0 * af) / 128.0,
        (7.0 + 18.0 * af) / 16.0,
        (-7.0 + 14.0 * af) / 32.0,
        (1.0 - 2.0 * af) / 16.0,
        (-1.0 + 2.0 * af) / 128.0,
    ]
    deriv = {1: 7.0 / 9.0, -1: -7.0 / 9.0, 2: 1.0 / 36.0, -2: -1.0 / 36.0}
    filt = {0: a[0]}
    for k in range(1, 5):
        filt[k] = a[k] / 2.0
        filt[-k] = a[k] / 2.0
    return deriv, filt


def operators(n, rows):
    total = n * rows
    result = []
    for alpha, stencil in zip(ALPHAS, stencils()):
        a = np.eye(total) + alpha * (np.eye(total, k=1) + np.eye(total, k=-1))
        b = sum(c * np.eye(total, k=k) for k, c in stencil.items())
        inverse = np.linalg.inv(a)
        dense = inverse @ b
        back, front = np.ones(total), np.ones(total)
        for k in range(1, total):
            front[k] = 1.0 - alpha * alpha / front[k - 1]
            back[total - 1 - k] = 1.0 - alpha * alpha / back[total - k]
        gain_l = np.prod((-alpha / back).reshape(n, rows), axis=1)
        gain_r = np.prod((-alpha / front).reshape(n, rows), axis=1)
        result.append((inverse, dense, gain_l, gain_r))
    return result


class Layout:
    def __init__(self):
        self.size = 0

    def take(self, count):
        at = self.size
        self.size += count
        return at


def coefficients(n, rows, radices):
    ops = operators(n, rows)
    lay = Layout()
    at = {
        "local": lay.take(2 * rows * rows),
        "ul": lay.take(2 * rows),
        "ur": lay.take(2 * rows),
        "er": lay.take(2 * HALO * HALO),
        "el": lay.take(2 * HALO * HALO),
        "sum": lay.take(4 * rows),
        "stage": [lay.take(4 + 8 * (r - 1)) for r in radices],
    }
    table = np.zeros((n, lay.size))
    for d in range(n):
        first, last = d * rows, d * rows + rows - 1
        line = table[d]
        for o, (inverse, dense, gain_l, gain_r) in enumerate(ops):
            own = dense[first : last + 1, first : last + 1]
            line[at["local"] + o * rows * rows :][: rows * rows] = own.reshape(-1)
            ul = inverse[first : last + 1, last]
            ur = inverse[first : last + 1, first]
            line[at["ul"] + o * rows :][:rows] = ul
            line[at["ur"] + o * rows :][:rows] = ur
            if d + 1 < n:
                nxt = slice(last + 1, last + 1 + rows)
                lam = dense[first, nxt] / inverse[first, last]
                table[d + 1, at["sum"] + (2 + o) * rows :][:rows] = lam
                for p in range(HALO):
                    for q in range(p + 1):
                        i = rows - HALO + p
                        value = dense[first + i, last + 1 + q] - ul[i] * lam[q]
                        line[at["er"] + (o * HALO + p) * HALO + q] = value
            if d > 0:
                prev = slice(first - rows, first)
                rho = dense[last, prev] / inverse[last, first]
                table[d - 1, at["sum"] + o * rows :][:rows] = rho
                for p in range(HALO):
                    for q in range(p, HALO):
                        j = rows - HALO + q
                        value = dense[first + p, first - rows + j] - ur[p] * rho[j]
                        line[at["el"] + (o * HALO + p) * HALO + q] = value
            stride = 1
            for s, radix in enumerate(radices):
                where = at["stage"][s]
                digit = (d // stride) % radix
                base = d - d % stride - digit * stride
                end = base + radix * stride
                start = base + digit * stride
                line[where + o] = np.prod(gain_r[start + stride : end])
                line[where + 2 + o] = np.prod(gain_l[base:start])
                for k in range(1, radix):
                    other = (digit - k) % radix
                    begin = base + other * stride
                    stop = begin + stride
                    slot = where + 4 + 8 * (k - 1)
                    if other < digit:
                        line[slot + o] = np.prod(gain_r[stop:d])
                    else:
                        line[slot + 2 + o] = np.prod(gain_l[d + 1 : begin])
                    line[slot + 4 + o] = np.prod(gain_r[stop:end])
                    line[slot + 6 + o] = np.prod(gain_l[base:begin])
                stride *= radix
    return table.astype(np.float32), at


def kernel(n, n_rad, radices, at, table_ref, f_ref, deriv_ref, filt_ref, radial_ref, *scratch):
    stages = len(radices)
    (tab, prefix, halo_l, halo_r, rim_l, rim_r, tab_sem, halo_send, halo_recv, rim_send, rim_recv) = scratch[:11]
    rest = scratch[11:]
    mine, came = rest[:stages], rest[stages : 2 * stages]
    sends, recvs = rest[2 * stages : 3 * stages], rest[3 * stages :]
    rows, fields, planes, width = f_ref.shape
    d = lax.axis_index("ax")
    r = lax.axis_index("rad")

    load = pltpu.make_async_copy(table_ref.at[d], tab, tab_sem)
    load.start()

    def const(index):
        return tab[0, index]

    def partner(s, k):
        stride = 1
        for radix in radices[:s]:
            stride *= radix
        digit = (d // stride) % radices[s]
        other = (digit + k) % radices[s]
        return digit, other, d + (other - digit) * stride

    barrier = pltpu.get_barrier_semaphore()
    fixed = 0
    for s in range(stages):
        for k in range(1, radices[s]):
            pl.semaphore_signal(barrier, inc=1, device_id={"ax": partner(s, k)[2]}, device_id_type=MESH)
            fixed += 1
    near = (
        (d > 0, {"ax": d - 1}),
        (d < n - 1, {"ax": d + 1}),
        (r > 0, {"rad": r - 1}),
        (r < n_rad - 1, {"rad": r + 1}),
    )
    for there, target in near:

        @pl.when(there)
        def _(target=target):
            pl.semaphore_signal(barrier, inc=1, device_id=target, device_id_type=MESH)

    load.wait()

    def sums(c, carry):
        own = [f_ref[j, c] for j in range(rows)]
        for u in range(4):
            acc = const(at["sum"] + u * rows) * own[0]
            for j in range(1, rows):
                acc = acc + const(at["sum"] + u * rows + j) * own[j]
            mine[0][c, u] = acc
        return carry

    lax.fori_loop(0, fields, sums, 0)

    beside = (d + n - 1) // n + (2 * n - 2 - d) // n
    across = (r + n_rad - 1) // n_rad + (2 * n_rad - 2 - r) // n_rad
    pl.semaphore_wait(barrier, fixed + beside + across)

    def stage_copy(s, k, c):
        digit, other, target = partner(s, k)
        if s == stages - 1:
            half = 1 - (other + radices[s] - digit) // radices[s]
            source = mine[s].at[c, pl.ds(2 * half, 2)]
        else:
            source = mine[s].at[c]
        return pltpu.make_async_remote_copy(
            src_ref=source,
            dst_ref=came[s].at[c, k - 1],
            send_sem=sends[s].at[c, k - 1],
            recv_sem=recvs[s].at[c, k - 1],
            device_id={"ax": target},
            device_id_type=MESH,
        )

    def to_right(c):
        return pltpu.make_async_remote_copy(
            src_ref=f_ref.at[pl.ds(rows - HALO, HALO), c],
            dst_ref=halo_l.at[c],
            send_sem=halo_send.at[0, c],
            recv_sem=halo_recv.at[0, c],
            device_id={"ax": d + 1},
            device_id_type=MESH,
        )

    def to_left(c):
        return pltpu.make_async_remote_copy(
            src_ref=f_ref.at[pl.ds(0, HALO), c],
            dst_ref=halo_r.at[c],
            send_sem=halo_send.at[1, c],
            recv_sem=halo_recv.at[1, c],
            device_id={"ax": d - 1},
            device_id_type=MESH,
        )

    rim_right = pltpu.make_async_remote_copy(
        src_ref=f_ref.at[:, :, :, pl.ds(width - EDGE, EDGE)],
        dst_ref=rim_l,
        send_sem=rim_send.at[0],
        recv_sem=rim_recv.at[0],
        device_id={"rad": r + 1},
        device_id_type=MESH,
    )
    rim_left = pltpu.make_async_remote_copy(
        src_ref=f_ref.at[:, :, :, pl.ds(0, EDGE)],
        dst_ref=rim_r,
        send_sem=rim_send.at[1],
        recv_sem=rim_recv.at[1],
        device_id={"rad": r - 1},
        device_id_type=MESH,
    )

    for c in range(fields):
        for k in range(1, radices[0]):
            stage_copy(0, k, c).start()

    @pl.when(r < n_rad - 1)
    def _():
        rim_right.start()

    @pl.when(r > 0)
    def _():
        rim_left.start()

    @pl.when(d < n - 1)
    def _():
        for c in range(fields):
            to_right(c).start()

    @pl.when(d > 0)
    def _():
        for c in range(fields):
            to_left(c).start()

    @pl.when(d == 0)
    def _():
        halo_l[...] = jnp.zeros_like(halo_l)

    @pl.when(d == n - 1)
    def _():
        halo_r[...] = jnp.zeros_like(halo_r)

    @pl.when(r == 0)
    def _():
        rim_l[...] = jnp.zeros_like(rim_l)

    @pl.when(r == n_rad - 1)
    def _():
        rim_r[...] = jnp.zeros_like(rim_r)

    def local(c, carry):
        own = [f_ref[j, c] for j in range(rows)]
        for o, out in enumerate((deriv_ref, filt_ref)):
            for i in range(rows):
                where = at["local"] + (o * rows + i) * rows
                acc = const(where) * own[0]
                for j in range(1, rows):
                    acc = acc + const(where + j) * own[j]
                out[i, c] = acc
        return carry

    lax.fori_loop(0, fields, local, 0)

    @pl.when(r < n_rad - 1)
    def _():
        rim_left.wait_recv()

    @pl.when(r > 0)
    def _():
        rim_right.wait_recv()

    def radial(c):
        def one(i, carry):
            wide = jnp.concatenate([rim_l[i, c], f_ref[i, c], rim_r[i, c]], axis=1)

            def cell(k):
                return wide[:, EDGE + k : EDGE + k + width]

            radial_ref[i, c] = (
                (45.0 / 60.0) * (cell(1) - cell(-1))
                - (9.0 / 60.0) * (cell(2) - cell(-2))
                + (1.0 / 60.0) * (cell(3) - cell(-3))
            )
            return carry

        lax.fori_loop(0, rows, one, 0)

    def step(s, c):
        final = s == stages - 1
        where = at["stage"][s]
        old = None if s == 0 else [prefix[c, u] for u in range(4)]
        grown = None if final else [const(where + u) * mine[s][c, u] for u in range(4)]
        for k in range(1, radices[s]):
            stage_copy(s, k, c).wait_recv()
            slot = where + 4 + 8 * (k - 1)
            got = [came[s][c, k - 1, u] for u in range(2 if final else 4)]
            if final:
                got = got + got
            add = [const(slot + u) * got[u] for u in range(4)]
            old = add if old is None else [a + b for a, b in zip(old, add)]
            if not final:
                grown = [g + const(slot + 4 + u) * got[u] for u, g in enumerate(grown)]
        for u in range(4):
            prefix[c, u] = old[u]
        if not final:
            for u in range(4):
                mine[s + 1][c, u] = grown[u]
            for k in range(1, radices[s + 1]):
                stage_copy(s + 1, k, c).start()

    for t in range(fields + stages - 1):
        for s in range(stages):
            if 0 <= t - s < fields:
                step(s, t - s)
        if t < fields:
            radial(t)

    for c in range(fields):

        @pl.when(d > 0)
        def _(c=c):
            to_right(c).wait_recv()

        @pl.when(d < n - 1)
        def _(c=c):
            to_left(c).wait_recv()

        pre = [prefix[c, u] for u in range(4)]
        left = [halo_l[c, q] for q in range(HALO)]
        right = [halo_r[c, q] for q in range(HALO)]
        for o, out in enumerate((deriv_ref, filt_ref)):
            reach = 1 if o == 0 else HALO
            for i in range(rows):
                acc = out[i, c] + const(at["ur"] + o * rows + i) * pre[o]
                acc = acc + const(at["ul"] + o * rows + i) * pre[2 + o]
                if i < reach:
                    for q in range(HALO - reach + i, HALO):
                        acc = acc + const(at["el"] + (o * HALO + i) * HALO + q) * left[q]
                p = i - (rows - HALO)
                if p >= HALO - reach:
                    for q in range(p - (HALO - reach) + 1):
                        acc = acc + const(at["er"] + (o * HALO + p) * HALO + q) * right[q]
                out[i, c] = acc

    for s in range(stages):
        for c in range(fields):
            for k in range(1, radices[s]):
                stage_copy(s, k, c).wait_send()

    @pl.when(d < n - 1)
    def _():
        for c in range(fields):
            to_right(c).wait_send()

    @pl.when(d > 0)
    def _():
        for c in range(fields):
            to_left(c).wait_send()

    @pl.when(r < n_rad - 1)
    def _():
        rim_right.wait_send()

    @pl.when(r > 0)
    def _():
        rim_left.wait_send()


def solution(mesh):
    n, n_rad = mesh.shape["ax"], mesh.shape["rad"]
    radices = stage_radices(n)

    def body(fields):
        rows, count, planes, width = fields.shape
        table, at = coefficients(n, rows, radices)
        size = table.shape[1]
        unit = (planes, width)
        last = len(radices) - 1
        dma = pltpu.SemaphoreType.DMA
        vmem = functools.partial(pltpu.VMEM, dtype=jnp.float32)
        scratch = [
            pltpu.SMEM((1, size), jnp.float32),
            vmem((count, 4) + unit),
            vmem((count, HALO) + unit),
            vmem((count, HALO) + unit),
            vmem((rows, count, planes, EDGE)),
            vmem((rows, count, planes, EDGE)),
            dma(()),
            dma((2, count)),
            dma((2, count)),
            dma((2,)),
            dma((2,)),
        ]
        scratch += [vmem((count, 4) + unit) for _ in radices]
        scratch += [vmem((count, k - 1, 2 if s == last else 4) + unit) for s, k in enumerate(radices)]
        scratch += [dma((count, k - 1)) for k in radices] * 2
        out = jax.ShapeDtypeStruct(fields.shape, jnp.float32)
        return pl.pallas_call(
            functools.partial(kernel, n, n_rad, radices, at),
            out_shape=(out, out, out),
            in_specs=[pl.BlockSpec(memory_space=pl.ANY), pl.BlockSpec(memory_space=pltpu.VMEM)],
            out_specs=(pl.BlockSpec(memory_space=pltpu.VMEM),) * 3,
            scratch_shapes=scratch,
            compiler_params=pltpu.CompilerParams(
                collective_id=0, has_side_effects=True, vmem_limit_bytes=40 * 1024 * 1024
            ),
        )(jnp.asarray(table).reshape(n, 1, size), fields)

    spec = P("ax", None, None, "rad")
    return jax.shard_map(body, mesh=mesh, in_specs=(spec,), out_specs=(spec,) * 3, check_vma=False)
```

```python
import functools

import jax
import jax.numpy as jnp
import numpy as np
from jax import lax
from jax.experimental import pallas as pl
from jax.experimental.pallas import tpu as pltpu
from jax.sharding import PartitionSpec as P

MESH = pl.DeviceIdType.MESH
ALPHAS = (1.0 / 3.0, 0.4999)
HALO = 3
EDGE = 128


def stage_radices(n):
    radices, m = [], n
    while m > 1:
        radix = next(k for k in range(2, m + 1) if m % k == 0)
        radices.append(radix)
        m //= radix
    return radices


def stencils():
    af = ALPHAS[1]
    a = [
        (93.0 + 70.0 * af) / 128.0,
        (7.0 + 18.0 * af) / 16.0,
        (-7.0 + 14.0 * af) / 32.0,
        (1.0 - 2.0 * af) / 16.0,
        (-1.0 + 2.0 * af) / 128.0,
    ]
    deriv = {1: 7.0 / 9.0, -1: -7.0 / 9.0, 2: 1.0 / 36.0, -2: -1.0 / 36.0}
    filt = {0: a[0]}
    for k in range(1, 5):
        filt[k] = a[k] / 2.0
        filt[-k] = a[k] / 2.0
    return deriv, filt


def operators(n, rows):
    total = n * rows
    result = []
    for alpha, stencil in zip(ALPHAS, stencils()):
        a = np.eye(total) + alpha * (np.eye(total, k=1) + np.eye(total, k=-1))
        b = sum(c * np.eye(total, k=k) for k, c in stencil.items())
        inverse = np.linalg.inv(a)
        dense = inverse @ b
        back, front = np.ones(total), np.ones(total)
        for k in range(1, total):
            front[k] = 1.0 - alpha * alpha / front[k - 1]
            back[total - 1 - k] = 1.0 - alpha * alpha / back[total - k]
        gain_l = np.prod((-alpha / back).reshape(n, rows), axis=1)
        gain_r = np.prod((-alpha / front).reshape(n, rows), axis=1)
        result.append((inverse, dense, gain_l, gain_r))
    return result


class Layout:
    def __init__(self):
        self.size = 0

    def take(self, count):
        at = self.size
        self.size += count
        return at


def coefficients(n, rows, radices):
    ops = operators(n, rows)
    lay = Layout()
    at = {
        "local": lay.take(2 * rows * rows),
        "ul": lay.take(2 * rows),
        "ur": lay.take(2 * rows),
        "er": lay.take(2 * HALO * HALO),
        "el": lay.take(2 * HALO * HALO),
        "sum": lay.take(4 * rows),
        "stage": [lay.take(4 + 8 * (r - 1)) for r in radices],
    }
    table = np.zeros((n, lay.size))
    for d in range(n):
        first, last = d * rows, d * rows + rows - 1
        line = table[d]
        for o, (inverse, dense, gain_l, gain_r) in enumerate(ops):
            own = dense[first : last + 1, first : last + 1]
            line[at["local"] + o * rows * rows :][: rows * rows] = own.reshape(-1)
            ul = inverse[first : last + 1, last]
            ur = inverse[first : last + 1, first]
            line[at["ul"] + o * rows :][:rows] = ul
            line[at["ur"] + o * rows :][:rows] = ur
            if d + 1 < n:
                nxt = slice(last + 1, last + 1 + rows)
                lam = dense[first, nxt] / inverse[first, last]
                table[d + 1, at["sum"] + (2 + o) * rows :][:rows] = lam
                for p in range(HALO):
                    for q in range(p + 1):
                        i = rows - HALO + p
                        value = dense[first + i, last + 1 + q] - ul[i] * lam[q]
                        line[at["er"] + (o * HALO + p) * HALO + q] = value
            if d > 0:
                prev = slice(first - rows, first)
                rho = dense[last, prev] / inverse[last, first]
                table[d - 1, at["sum"] + o * rows :][:rows] = rho
                for p in range(HALO):
                    for q in range(p, HALO):
                        j = rows - HALO + q
                        value = dense[first + p, first - rows + j] - ur[p] * rho[j]
                        line[at["el"] + (o * HALO + p) * HALO + q] = value
            stride = 1
            for s, radix in enumerate(radices):
                where = at["stage"][s]
                digit = (d // stride) % radix
                base = d - d % stride - digit * stride
                end = base + radix * stride
                start = base + digit * stride
                line[where + o] = np.prod(gain_r[start + stride : end])
                line[where + 2 + o] = np.prod(gain_l[base:start])
                for k in range(1, radix):
                    other = (digit - k) % radix
                    begin = base + other * stride
                    stop = begin + stride
                    slot = where + 4 + 8 * (k - 1)
                    if other < digit:
                        line[slot + o] = np.prod(gain_r[stop:d])
                    else:
                        line[slot + 2 + o] = np.prod(gain_l[d + 1 : begin])
                    line[slot + 4 + o] = np.prod(gain_r[stop:end])
                    line[slot + 6 + o] = np.prod(gain_l[base:begin])
                stride *= radix
    return table.astype(np.float32), at


def kernel(n, n_rad, radices, at, table_ref, fields_ref, deriv_ref, filt_ref, radial_ref, *scratch):
    stages = len(radices)
    (f_ref, tab, prefix, halo_l, halo_r, rim_l, rim_r) = scratch[:7]
    (f_sem, tab_sem, halo_send, halo_recv, rim_send, rim_recv) = scratch[7:13]
    rest = scratch[13:]
    mine, came = rest[:stages], rest[stages : 2 * stages]
    sends, recvs = rest[2 * stages : 3 * stages], rest[3 * stages :]
    rows, fields, planes, width = f_ref.shape
    d = lax.axis_index("ax")
    r = lax.axis_index("rad")

    load = pltpu.make_async_copy(table_ref.at[d], tab, tab_sem)
    load.start()

    def fetch(c):
        return pltpu.make_async_copy(fields_ref.at[:, c], f_ref.at[:, c], f_sem.at[c])

    for c in range(fields):
        fetch(c).start()

    def const(index):
        return tab[0, index]

    def partner(s, k):
        stride = 1
        for radix in radices[:s]:
            stride *= radix
        digit = (d // stride) % radices[s]
        other = (digit + k) % radices[s]
        return digit, other, d + (other - digit) * stride

    barrier = pltpu.get_barrier_semaphore()
    fixed = 0
    for s in range(stages):
        for k in range(1, radices[s]):
            pl.semaphore_signal(barrier, inc=1, device_id={"ax": partner(s, k)[2]}, device_id_type=MESH)
            fixed += 1
    near = (
        (d > 0, {"ax": d - 1}),
        (d < n - 1, {"ax": d + 1}),
        (r > 0, {"rad": r - 1}),
        (r < n_rad - 1, {"rad": r + 1}),
    )
    for there, target in near:

        @pl.when(there)
        def _(target=target):
            pl.semaphore_signal(barrier, inc=1, device_id=target, device_id_type=MESH)

    @pl.when(d == 0)
    def _():
        halo_l[...] = jnp.zeros_like(halo_l)

    @pl.when(d == n - 1)
    def _():
        halo_r[...] = jnp.zeros_like(halo_r)

    @pl.when(r == 0)
    def _():
        rim_l[...] = jnp.zeros_like(rim_l)

    @pl.when(r == n_rad - 1)
    def _():
        rim_r[...] = jnp.zeros_like(rim_r)

    load.wait()

    def sums(c, carry):
        fetch(c).wait()
        own = [f_ref[j, c] for j in range(rows)]
        for u in range(4):
            acc = const(at["sum"] + u * rows) * own[0]
            for j in range(1, rows):
                acc = acc + const(at["sum"] + u * rows + j) * own[j]
            mine[0][c, u] = acc
        return carry

    lax.fori_loop(0, fields, sums, 0)

    beside = (d + n - 1) // n + (2 * n - 2 - d) // n
    across = (r + n_rad - 1) // n_rad + (2 * n_rad - 2 - r) // n_rad
    pl.semaphore_wait(barrier, fixed + beside + across)

    def stage_copy(s, k, c):
        digit, other, target = partner(s, k)
        if s == stages - 1:
            half = 1 - (other + radices[s] - digit) // radices[s]
            source = mine[s].at[c, pl.ds(2 * half, 2)]
        else:
            source = mine[s].at[c]
        return pltpu.make_async_remote_copy(
            src_ref=source,
            dst_ref=came[s].at[c, k - 1],
            send_sem=sends[s].at[c, k - 1],
            recv_sem=recvs[s].at[c, k - 1],
            device_id={"ax": target},
            device_id_type=MESH,
        )

    def to_right(c):
        return pltpu.make_async_remote_copy(
            src_ref=f_ref.at[pl.ds(rows - HALO, HALO), c],
            dst_ref=halo_l.at[c],
            send_sem=halo_send.at[0, c],
            recv_sem=halo_recv.at[0, c],
            device_id={"ax": d + 1},
            device_id_type=MESH,
        )

    def to_left(c):
        return pltpu.make_async_remote_copy(
            src_ref=f_ref.at[pl.ds(0, HALO), c],
            dst_ref=halo_r.at[c],
            send_sem=halo_send.at[1, c],
            recv_sem=halo_recv.at[1, c],
            device_id={"ax": d - 1},
            device_id_type=MESH,
        )

    rim_right = pltpu.make_async_remote_copy(
        src_ref=f_ref.at[:, :, :, pl.ds(width - EDGE, EDGE)],
        dst_ref=rim_l,
        send_sem=rim_send.at[0],
        recv_sem=rim_recv.at[0],
        device_id={"rad": r + 1},
        device_id_type=MESH,
    )
    rim_left = pltpu.make_async_remote_copy(
        src_ref=f_ref.at[:, :, :, pl.ds(0, EDGE)],
        dst_ref=rim_r,
        send_sem=rim_send.at[1],
        recv_sem=rim_recv.at[1],
        device_id={"rad": r - 1},
        device_id_type=MESH,
    )

    @pl.when(r < n_rad - 1)
    def _():
        rim_right.start()

    @pl.when(r > 0)
    def _():
        rim_left.start()

    for c in range(fields):
        for k in range(1, radices[0]):
            stage_copy(0, k, c).start()

    def local(c, carry):
        own = [f_ref[j, c] for j in range(rows)]
        for o, out in enumerate((deriv_ref, filt_ref)):
            for i in range(rows):
                where = at["local"] + (o * rows + i) * rows
                acc = const(where) * own[0]
                for j in range(1, rows):
                    acc = acc + const(where + j) * own[j]
                out[i, c] = acc
        return carry

    lax.fori_loop(0, fields, local, 0)

    def radial(c):
        def one(i, carry):
            wide = jnp.concatenate([rim_l[i, c], f_ref[i, c], rim_r[i, c]], axis=1)

            def cell(k):
                return wide[:, EDGE + k : EDGE + k + width]

            radial_ref[i, c] = (
                (45.0 / 60.0) * (cell(1) - cell(-1))
                - (9.0 / 60.0) * (cell(2) - cell(-2))
                + (1.0 / 60.0) * (cell(3) - cell(-3))
            )
            return carry

        lax.fori_loop(0, rows, one, 0)

    def step(s, c):
        final = s == stages - 1
        where = at["stage"][s]
        old = None if s == 0 else [prefix[c, u] for u in range(4)]
        grown = None if final else [const(where + u) * mine[s][c, u] for u in range(4)]
        for k in range(1, radices[s]):
            stage_copy(s, k, c).wait_recv()
            slot = where + 4 + 8 * (k - 1)
            got = [came[s][c, k - 1, u] for u in range(2 if final else 4)]
            if final:
                got = got + got
            add = [const(slot + u) * got[u] for u in range(4)]
            old = add if old is None else [a + b for a, b in zip(old, add)]
            if not final:
                grown = [g + const(slot + 4 + u) * got[u] for u, g in enumerate(grown)]
        for u in range(4):
            prefix[c, u] = old[u]
        if not final:
            for u in range(4):
                mine[s + 1][c, u] = grown[u]
            for k in range(1, radices[s + 1]):
                stage_copy(s + 1, k, c).start()

    def halos(c):
        @pl.when(d < n - 1)
        def _():
            to_right(c).start()

        @pl.when(d > 0)
        def _():
            to_left(c).start()

    for t in range(fields + stages - 1):
        for s in range(stages):
            if 0 <= t - s < fields:
                step(s, t - s)
        if t < fields:
            halos(t)
        if t == 0:

            @pl.when(r < n_rad - 1)
            def _():
                rim_left.wait_recv()

            @pl.when(r > 0)
            def _():
                rim_right.wait_recv()

        if t < fields:
            radial(t)

    for c in range(fields):

        @pl.when(d > 0)
        def _(c=c):
            to_right(c).wait_recv()

        @pl.when(d < n - 1)
        def _(c=c):
            to_left(c).wait_recv()

        pre = [prefix[c, u] for u in range(4)]
        left = [halo_l[c, q] for q in range(HALO)]
        right = [halo_r[c, q] for q in range(HALO)]
        for o, out in enumerate((deriv_ref, filt_ref)):
            reach = 1 if o == 0 else HALO
            for i in range(rows):
                acc = out[i, c] + const(at["ur"] + o * rows + i) * pre[o]
                acc = acc + const(at["ul"] + o * rows + i) * pre[2 + o]
                if i < reach:
                    for q in range(HALO - reach + i, HALO):
                        acc = acc + const(at["el"] + (o * HALO + i) * HALO + q) * left[q]
                p = i - (rows - HALO)
                if p >= HALO - reach:
                    for q in range(p - (HALO - reach) + 1):
                        acc = acc + const(at["er"] + (o * HALO + p) * HALO + q) * right[q]
                out[i, c] = acc

    for s in range(stages):
        for c in range(fields):
            for k in range(1, radices[s]):
                stage_copy(s, k, c).wait_send()

    @pl.when(d < n - 1)
    def _():
        for c in range(fields):
            to_right(c).wait_send()

    @pl.when(d > 0)
    def _():
        for c in range(fields):
            to_left(c).wait_send()

    @pl.when(r < n_rad - 1)
    def _():
        rim_right.wait_send()

    @pl.when(r > 0)
    def _():
        rim_left.wait_send()


def store(a, b, c, out_a, out_b, out_c, sem):
    copies = [
        pltpu.make_async_copy(src, dst, sem.at[i])
        for i, (src, dst) in enumerate(((a, out_a), (b, out_b), (c, out_c)))
    ]
    for copy in copies:
        copy.start()
    for copy in copies:
        copy.wait()


def solution(mesh):
    n, n_rad = mesh.shape["ax"], mesh.shape["rad"]
    radices = stage_radices(n)

    def body(fields):
        rows, count, planes, width = fields.shape
        table, at = coefficients(n, rows, radices)
        size = table.shape[1]
        unit = (planes, width)
        last = len(radices) - 1
        dma = pltpu.SemaphoreType.DMA
        vmem = functools.partial(pltpu.VMEM, dtype=jnp.float32)
        scratch = [
            vmem(fields.shape),
            pltpu.SMEM((1, size), jnp.float32),
            vmem((count, 4) + unit),
            vmem((count, HALO) + unit),
            vmem((count, HALO) + unit),
            vmem((rows, count, planes, EDGE)),
            vmem((rows, count, planes, EDGE)),
            dma((count,)),
            dma(()),
            dma((2, count)),
            dma((2, count)),
            dma((2,)),
            dma((2,)),
        ]
        scratch += [vmem((count, 4) + unit) for _ in radices]
        scratch += [vmem((count, k - 1, 2 if s == last else 4) + unit) for s, k in enumerate(radices)]
        scratch += [dma((count, k - 1)) for k in radices] * 2
        out = jax.ShapeDtypeStruct(fields.shape, jnp.float32)
        solved = pl.pallas_call(
            functools.partial(kernel, n, n_rad, radices, at),
            out_shape=(out, out, out),
            in_specs=[pl.BlockSpec(memory_space=pltpu.HBM)] * 2,
            out_specs=(pl.BlockSpec(memory_space=pltpu.VMEM),) * 3,
            scratch_shapes=scratch,
            compiler_params=pltpu.CompilerParams(
                collective_id=0, has_side_effects=True, vmem_limit_bytes=40 * 1024 * 1024
            ),
        )(jnp.asarray(table).reshape(n, 1, size), fields)
        return pl.pallas_call(
            store,
            out_shape=(out, out, out),
            in_specs=[pl.BlockSpec(memory_space=pltpu.VMEM)] * 3,
            out_specs=(pl.BlockSpec(memory_space=pltpu.HBM),) * 3,
            scratch_shapes=[dma((3,))],
            compiler_params=pltpu.CompilerParams(vmem_limit_bytes=4 * 1024 * 1024),
        )(*solved)

    spec = P("ax", None, None, "rad")
    return jax.shard_map(body, mesh=mesh, in_specs=(spec,), out_specs=(spec,) * 3, check_vma=False)
```

```python
import functools

import jax
import jax.numpy as jnp
import numpy as np
from jax import lax
from jax.experimental import pallas as pl
from jax.experimental.pallas import tpu as pltpu
from jax.sharding import PartitionSpec as P

MESH = pl.DeviceIdType.MESH
ALPHAS = (1.0 / 3.0, 0.4999)
HALO = 3
EDGE = 128
SPLIT = 1
SKEW = 2.0
HALO_AT = 0.1
LOCAL_AT = -5.0
RADIAL_AT = 1.2


def stage_radices(n):
    radices, m = [], n
    while m > 1:
        radix = next(k for k in range(2, m + 1) if m % k == 0)
        radices.append(radix)
        m //= radix
    return radices


def stencils():
    af = ALPHAS[1]
    a = [
        (93.0 + 70.0 * af) / 128.0,
        (7.0 + 18.0 * af) / 16.0,
        (-7.0 + 14.0 * af) / 32.0,
        (1.0 - 2.0 * af) / 16.0,
        (-1.0 + 2.0 * af) / 128.0,
    ]
    deriv = {1: 7.0 / 9.0, -1: -7.0 / 9.0, 2: 1.0 / 36.0, -2: -1.0 / 36.0}
    filt = {0: a[0]}
    for k in range(1, 5):
        filt[k] = a[k] / 2.0
        filt[-k] = a[k] / 2.0
    return deriv, filt


def operators(n, rows):
    total = n * rows
    result = []
    for alpha, stencil in zip(ALPHAS, stencils()):
        a = np.eye(total) + alpha * (np.eye(total, k=1) + np.eye(total, k=-1))
        b = sum(c * np.eye(total, k=k) for k, c in stencil.items())
        inverse = np.linalg.inv(a)
        dense = inverse @ b
        back, front = np.ones(total), np.ones(total)
        for k in range(1, total):
            front[k] = 1.0 - alpha * alpha / front[k - 1]
            back[total - 1 - k] = 1.0 - alpha * alpha / back[total - k]
        gain_l = np.prod((-alpha / back).reshape(n, rows), axis=1)
        gain_r = np.prod((-alpha / front).reshape(n, rows), axis=1)
        result.append((inverse, dense, gain_l, gain_r))
    return result


class Layout:
    def __init__(self):
        self.size = 0

    def take(self, count):
        at = self.size
        self.size += count
        return at


def coefficients(n, rows, radices):
    ops = operators(n, rows)
    lay = Layout()
    at = {
        "local": lay.take(2 * rows * rows),
        "ul": lay.take(2 * rows),
        "ur": lay.take(2 * rows),
        "er": lay.take(2 * HALO * HALO),
        "el": lay.take(2 * HALO * HALO),
        "sum": lay.take(4 * rows),
        "stage": [lay.take(4 + 8 * (r - 1)) for r in radices],
    }
    table = np.zeros((n, lay.size))
    for d in range(n):
        first, last = d * rows, d * rows + rows - 1
        line = table[d]
        for o, (inverse, dense, gain_l, gain_r) in enumerate(ops):
            own = dense[first : last + 1, first : last + 1]
            line[at["local"] + o * rows * rows :][: rows * rows] = own.reshape(-1)
            ul = inverse[first : last + 1, last]
            ur = inverse[first : last + 1, first]
            line[at["ul"] + o * rows :][:rows] = ul
            line[at["ur"] + o * rows :][:rows] = ur
            if d + 1 < n:
                nxt = slice(last + 1, last + 1 + rows)
                lam = dense[first, nxt] / inverse[first, last]
                table[d + 1, at["sum"] + (2 + o) * rows :][:rows] = lam
                for p in range(HALO):
                    for q in range(p + 1):
                        i = rows - HALO + p
                        value = dense[first + i, last + 1 + q] - ul[i] * lam[q]
                        line[at["er"] + (o * HALO + p) * HALO + q] = value
            if d > 0:
                prev = slice(first - rows, first)
                rho = dense[last, prev] / inverse[last, first]
                table[d - 1, at["sum"] + o * rows :][:rows] = rho
                for p in range(HALO):
                    for q in range(p, HALO):
                        j = rows - HALO + q
                        value = dense[first + p, first - rows + j] - ur[p] * rho[j]
                        line[at["el"] + (o * HALO + p) * HALO + q] = value
            stride = 1
            for s, radix in enumerate(radices):
                where = at["stage"][s]
                digit = (d // stride) % radix
                base = d - d % stride - digit * stride
                end = base + radix * stride
                start = base + digit * stride
                line[where + o] = np.prod(gain_r[start + stride : end])
                line[where + 2 + o] = np.prod(gain_l[base:start])
                for k in range(1, radix):
                    other = (digit - k) % radix
                    begin = base + other * stride
                    stop = begin + stride
                    slot = where + 4 + 8 * (k - 1)
                    if other < digit:
                        line[slot + o] = np.prod(gain_r[stop:d])
                    else:
                        line[slot + 2 + o] = np.prod(gain_l[d + 1 : begin])
                    line[slot + 4 + o] = np.prod(gain_r[stop:end])
                    line[slot + 6 + o] = np.prod(gain_l[base:begin])
                stride *= radix
    return table.astype(np.float32), at


def kernel(n, n_rad, radices, at, table_ref, f_ref, deriv_ref, filt_ref, radial_ref, *scratch):
    stages = len(radices)
    (tab, prefix, halo_l, halo_r, rim_l, rim_r) = scratch[:6]
    (tab_sem, halo_send, halo_recv, rim_send, rim_recv) = scratch[6:11]
    rest = scratch[11:]
    mine, came = rest[:stages], rest[stages : 2 * stages]
    sends, recvs = rest[2 * stages : 3 * stages], rest[3 * stages :]
    rows, fields, planes, width = f_ref.shape
    pieces = fields * SPLIT
    part = width // SPLIT
    lanes = [slice(h * part, (h + 1) * part) for h in range(SPLIT)]
    d = lax.axis_index("ax")
    r = lax.axis_index("rad")

    load = pltpu.make_async_copy(table_ref.at[d], tab, tab_sem)
    load.start()

    def const(index):
        return tab[0, index]

    def partner(s, k):
        stride = 1
        for radix in radices[:s]:
            stride *= radix
        digit = (d // stride) % radices[s]
        other = (digit + k) % radices[s]
        return digit, other, d + (other - digit) * stride

    barrier = pltpu.get_barrier_semaphore()
    fixed = 0
    for s in range(stages):
        for k in range(1, radices[s]):
            pl.semaphore_signal(barrier, inc=1, device_id={"ax": partner(s, k)[2]}, device_id_type=MESH)
            fixed += 1
    near = (
        (d > 0, {"ax": d - 1}),
        (d < n - 1, {"ax": d + 1}),
        (r > 0, {"rad": r - 1}),
        (r < n_rad - 1, {"rad": r + 1}),
    )
    for there, target in near:

        @pl.when(there)
        def _(target=target):
            pl.semaphore_signal(barrier, inc=1, device_id=target, device_id_type=MESH)

    @pl.when(d == 0)
    def _():
        halo_l[...] = jnp.zeros_like(halo_l)

    @pl.when(d == n - 1)
    def _():
        halo_r[...] = jnp.zeros_like(halo_r)

    @pl.when(r == 0)
    def _():
        rim_l[...] = jnp.zeros_like(rim_l)

    @pl.when(r == n_rad - 1)
    def _():
        rim_r[...] = jnp.zeros_like(rim_r)

    load.wait()

    def sums(c, carry):
        own = [f_ref[j, c] for j in range(rows)]
        for u in range(4):
            acc = const(at["sum"] + u * rows) * own[0]
            for j in range(1, rows):
                acc = acc + const(at["sum"] + u * rows + j) * own[j]
            for h in range(SPLIT):
                mine[0][c * SPLIT + h, u] = acc[:, lanes[h]]
        return carry

    lax.fori_loop(0, fields, sums, 0)

    beside = (d + n - 1) // n + (2 * n - 2 - d) // n
    across = (r + n_rad - 1) // n_rad + (2 * n_rad - 2 - r) // n_rad
    pl.semaphore_wait(barrier, fixed + beside + across)

    def stage_copy(s, k, c):
        digit, other, target = partner(s, k)
        if s == stages - 1:
            half = 1 - (other + radices[s] - digit) // radices[s]
            source = mine[s].at[c, pl.ds(2 * half, 2)]
        else:
            source = mine[s].at[c]
        return pltpu.make_async_remote_copy(
            src_ref=source,
            dst_ref=came[s].at[c, k - 1],
            send_sem=sends[s].at[c, k - 1],
            recv_sem=recvs[s].at[c, k - 1],
            device_id={"ax": target},
            device_id_type=MESH,
        )

    def to_right(c):
        return pltpu.make_async_remote_copy(
            src_ref=f_ref.at[pl.ds(rows - HALO, HALO), c],
            dst_ref=halo_l.at[c],
            send_sem=halo_send.at[0, c],
            recv_sem=halo_recv.at[0, c],
            device_id={"ax": d + 1},
            device_id_type=MESH,
        )

    def to_left(c):
        return pltpu.make_async_remote_copy(
            src_ref=f_ref.at[pl.ds(0, HALO), c],
            dst_ref=halo_r.at[c],
            send_sem=halo_send.at[1, c],
            recv_sem=halo_recv.at[1, c],
            device_id={"ax": d - 1},
            device_id_type=MESH,
        )

    rim_right = pltpu.make_async_remote_copy(
        src_ref=f_ref.at[:, :, :, pl.ds(width - EDGE, EDGE)],
        dst_ref=rim_l,
        send_sem=rim_send.at[0],
        recv_sem=rim_recv.at[0],
        device_id={"rad": r + 1},
        device_id_type=MESH,
    )
    rim_left = pltpu.make_async_remote_copy(
        src_ref=f_ref.at[:, :, :, pl.ds(0, EDGE)],
        dst_ref=rim_r,
        send_sem=rim_send.at[1],
        recv_sem=rim_recv.at[1],
        device_id={"rad": r - 1},
        device_id_type=MESH,
    )

    @pl.when(r < n_rad - 1)
    def _():
        rim_right.start()

    @pl.when(r > 0)
    def _():
        rim_left.start()

    for c in range(pieces):
        for k in range(1, radices[0]):
            stage_copy(0, k, c).start()

    def local(c, carry):
        own = [f_ref[j, c] for j in range(rows)]
        for o, out in enumerate((deriv_ref, filt_ref)):
            for i in range(rows):
                where = at["local"] + (o * rows + i) * rows
                acc = const(where) * own[0]
                for j in range(1, rows):
                    acc = acc + const(where + j) * own[j]
                out[i, c] = acc
        return carry

    def local_part(c):
        lax.fori_loop(c, c + 1, local, 0)

    def radial(c):
        def one(i, carry):
            wide = jnp.concatenate([rim_l[i, c], f_ref[i, c], rim_r[i, c]], axis=1)

            def cell(k):
                return wide[:, EDGE + k : EDGE + k + width]

            radial_ref[i, c] = (
                (45.0 / 60.0) * (cell(1) - cell(-1))
                - (9.0 / 60.0) * (cell(2) - cell(-2))
                + (1.0 / 60.0) * (cell(3) - cell(-3))
            )
            return carry

        lax.fori_loop(0, rows, one, 0)

    def step(s, c):
        final = s == stages - 1
        where = at["stage"][s]
        old = None if s == 0 else [prefix[c, u] for u in range(4)]
        grown = None if final else [const(where + u) * mine[s][c, u] for u in range(4)]
        for k in range(1, radices[s]):
            stage_copy(s, k, c).wait_recv()
            slot = where + 4 + 8 * (k - 1)
            got = [came[s][c, k - 1, u] for u in range(2 if final else 4)]
            if final:
                got = got + got
            add = [const(slot + u) * got[u] for u in range(4)]
            old = add if old is None else [a + b for a, b in zip(old, add)]
            if not final:
                grown = [g + const(slot + 4 + u) * got[u] for u, g in enumerate(grown)]
        for u in range(4):
            prefix[c, u] = old[u]
        if not final:
            for u in range(4):
                mine[s + 1][c, u] = grown[u]
            for k in range(1, radices[s + 1]):
                stage_copy(s + 1, k, c).start()

    def halos(c):
        @pl.when(d < n - 1)
        def _():
            to_right(c).start()

        @pl.when(d > 0)
        def _():
            to_left(c).start()

    def rim_wait():
        @pl.when(r < n_rad - 1)
        def _():
            rim_left.wait_recv()

        @pl.when(r > 0)
        def _():
            rim_right.wait_recv()

    events = [(c / SPLIT + SKEW * s, functools.partial(step, s, c)) for s in range(stages) for c in range(pieces)]
    events += [(c + HALO_AT, functools.partial(halos, c)) for c in range(fields)]
    events += [(c + LOCAL_AT, functools.partial(local_part, c)) for c in range(fields)]
    events += [(c + RADIAL_AT, functools.partial(radial, c)) for c in range(fields)]
    events.append((RADIAL_AT - 0.01, rim_wait))
    for _, event in sorted(events, key=lambda item: item[0]):
        event()

    for c in range(fields):

        @pl.when(d > 0)
        def _(c=c):
            to_right(c).wait_recv()

        @pl.when(d < n - 1)
        def _(c=c):
            to_left(c).wait_recv()

        for h, cut in enumerate(lanes):
            pre = [prefix[c * SPLIT + h, u] for u in range(4)]
            left = [halo_l[c, q, :, cut] for q in range(HALO)]
            right = [halo_r[c, q, :, cut] for q in range(HALO)]
            for o, out in enumerate((deriv_ref, filt_ref)):
                reach = 1 if o == 0 else HALO
                for i in range(rows):
                    acc = out[i, c, :, cut] + const(at["ur"] + o * rows + i) * pre[o]
                    acc = acc + const(at["ul"] + o * rows + i) * pre[2 + o]
                    if i < reach:
                        for q in range(HALO - reach + i, HALO):
                            acc = acc + const(at["el"] + (o * HALO + i) * HALO + q) * left[q]
                    p = i - (rows - HALO)
                    if p >= HALO - reach:
                        for q in range(p - (HALO - reach) + 1):
                            acc = acc + const(at["er"] + (o * HALO + p) * HALO + q) * right[q]
                    out[i, c, :, cut] = acc

    for s in range(stages):
        for c in range(pieces):
            for k in range(1, radices[s]):
                stage_copy(s, k, c).wait_send()

    @pl.when(d < n - 1)
    def _():
        for c in range(fields):
            to_right(c).wait_send()

    @pl.when(d > 0)
    def _():
        for c in range(fields):
            to_left(c).wait_send()

    @pl.when(r < n_rad - 1)
    def _():
        rim_right.wait_send()

    @pl.when(r > 0)
    def _():
        rim_left.wait_send()


def store(a, b, c, out_a, out_b, out_c, sem):
    copies = [
        pltpu.make_async_copy(src, dst, sem.at[i])
        for i, (src, dst) in enumerate(((a, out_a), (b, out_b), (c, out_c)))
    ]
    for copy in copies:
        copy.start()
    for copy in copies:
        copy.wait()


def solution(mesh):
    n, n_rad = mesh.shape["ax"], mesh.shape["rad"]
    radices = stage_radices(n)

    def body(fields):
        rows, count, planes, width = fields.shape
        table, at = coefficients(n, rows, radices)
        size = table.shape[1]
        whole, unit, pieces = (planes, width), (planes, width // SPLIT), count * SPLIT
        last = len(radices) - 1
        dma = pltpu.SemaphoreType.DMA
        vmem = functools.partial(pltpu.VMEM, dtype=jnp.float32)
        scratch = [
            pltpu.SMEM((1, size), jnp.float32),
            vmem((pieces, 4) + unit),
            vmem((count, HALO) + whole),
            vmem((count, HALO) + whole),
            vmem((rows, count, planes, EDGE)),
            vmem((rows, count, planes, EDGE)),
            dma(()),
            dma((2, count)),
            dma((2, count)),
            dma((2,)),
            dma((2,)),
        ]
        scratch += [vmem((pieces, 4) + unit) for _ in radices]
        scratch += [vmem((pieces, k - 1, 2 if s == last else 4) + unit) for s, k in enumerate(radices)]
        scratch += [dma((pieces, k - 1)) for k in radices] * 2
        out = jax.ShapeDtypeStruct(fields.shape, jnp.float32)
        solved = pl.pallas_call(
            functools.partial(kernel, n, n_rad, radices, at),
            out_shape=(out, out, out),
            in_specs=[pl.BlockSpec(memory_space=pltpu.HBM), pl.BlockSpec(memory_space=pltpu.VMEM)],
            out_specs=(pl.BlockSpec(memory_space=pltpu.VMEM),) * 3,
            scratch_shapes=scratch,
            compiler_params=pltpu.CompilerParams(
                collective_id=0, has_side_effects=True, vmem_limit_bytes=40 * 1024 * 1024
            ),
        )(jnp.asarray(table).reshape(n, 1, size), fields)
        return pl.pallas_call(
            store,
            out_shape=(out, out, out),
            in_specs=[pl.BlockSpec(memory_space=pltpu.VMEM)] * 3,
            out_specs=(pl.BlockSpec(memory_space=pltpu.HBM),) * 3,
            scratch_shapes=[dma((3,))],
            compiler_params=pltpu.CompilerParams(vmem_limit_bytes=4 * 1024 * 1024),
        )(*solved)

    spec = P("ax", None, None, "rad")
    return jax.shard_map(body, mesh=mesh, in_specs=(spec,), out_specs=(spec,) * 3, check_vma=False)
```
